32 devices in a mesh: rot: 4 (over y, x), space: 8 (over z, core).
Axes of the slice: x: 2, y: 2, z: 4, core: 2. Of those that a mesh axis runs over, the one named last changes fastest.
Arguments:
- raster: bfloat16 [4, 128, 2, 256], P(None, 'space'), may hold values from -6 to 6
- coarse_features: bfloat16 [4, 64, 128, 2, 256], P('rot', None, 'space'), may hold values from -6 to 6
- lift_weight: bfloat16 [4, 9, 64, 4], P('rot'), may hold values from -1 to 1
- lift_bias: float32 [64], replicated, may hold values from -3 to 3
- group_weight: bfloat16 [4, 9, 64, 64], P('rot'), may hold values from -0.125 to 0.125
- group_bias: float32 [64], replicated, may hold values from -3 to 3
Outputs:
- features: bfloat16 [4, 64, 128, 2, 256], P('rot', None, 'space')
The draws below stay inside these ranges and needn't reach their ends.
All inputs are finite; a program needn't handle non-finite values.
Results may differ from the reference program's by a relative error of at most 0.0045.
Values may be sent and summed in bfloat16 or wider, within the bound.
A program may use at most 192 MiB of HBM per device.

```python
import jax
import jax.numpy as jnp
import numpy as np
from jax import lax

C = 64
CIN = 4
COLS = 256
TILES = 2
ROTS = 4
HEIGHT = 128


def block_scale(rng, extent, cuts, smallest, top_value):
    def one(axis_at, shards_of):
        draws = jax.random.uniform(jax.random.fold_in(jax.random.fold_in(rng, 6), axis_at), (shards_of,), jnp.float32, smallest / len(cuts), top_value / len(cuts))
        return jnp.repeat(jnp.exp(draws), extent[axis_at] // shards_of).reshape((-1,) + (1,) * (len(extent) - axis_at - 1))

    loudness = one(*cuts[0])
    for cut in cuts[1:]:
        loudness = loudness * one(*cut)
    return loudness


def gaussian(key, shape, deviation, most, split=(), dtype=jnp.bfloat16):
    gain = block_scale(key, shape, split, -0.22, 0.18) if split else 1.0
    result = jax.random.normal(key, shape, jnp.float32) * deviation * gain
    return jnp.minimum(jnp.maximum(result, -most), most).astype(dtype)


def setup_inputs(seed: int = 0) -> dict:
    key_of = jax.random.split(jax.random.key(seed), 7)
    return {
        "raster": gaussian(key_of[0], (CIN, HEIGHT, TILES, COLS), 1.0, 6.0, ((1, 8),)),
        "coarse_features": gaussian(key_of[1], (ROTS, C, HEIGHT, TILES, COLS), 1.0, 6.0, ((0, 4), (2, 8))),
        "lift_weight": gaussian(key_of[2], (ROTS, 9, C, CIN), (9 * CIN) ** -0.5, 1.0, ((0, 4),)),
        "lift_bias": gaussian(key_of[3], (C,), 0.5, 3.0, (), jnp.float32),
        "group_weight": gaussian(key_of[4], (ROTS, 9, C, C), (9 * C * ROTS) ** -0.5, 0.125, ((0, 4),)),
        "group_bias": gaussian(key_of[5], (C,), 0.5, 3.0, (), jnp.float32),
    }


def conv_full(images, kernel):
    return lax.conv_general_dilated(images, kernel, (1, 1), ((1, 1), (1, 1)), dimension_numbers=("NCHW", "OIHW", "NCHW"), precision=lax.Precision.HIGHEST)


def reference(raster, coarse_features, lift_weight, lift_bias, group_weight, group_bias):
    rotations = lift_weight.shape[0]
    channels = lift_weight.shape[2]
    images = jnp.transpose(raster.astype(jnp.float32), (2, 0, 1, 3))
    tile_count = images.shape[0]
    row_total = images.shape[2]
    col_total = images.shape[3]
    lift_kernel = jnp.transpose(lift_weight.astype(jnp.float32).reshape(rotations, 3, 3, channels, -1), (0, 3, 4, 1, 2)).reshape(rotations * channels, -1, 3, 3)
    lifted = conv_full(images, lift_kernel).reshape(tile_count, rotations, channels, row_total, col_total)
    coarse = jnp.transpose(coarse_features.astype(jnp.float32), (3, 0, 1, 2, 4))
    hidden = jnp.maximum(lifted + lift_bias[None, None, :, None, None] + coarse, 0.0).astype(jnp.bfloat16)
    hidden = lax.optimization_barrier(hidden)
    relative = (np.arange(rotations)[:, None] - np.arange(rotations)[None, :]) % rotations
    filter_bank = group_weight.astype(jnp.float32)[relative]
    filter_bank = filter_bank.reshape(rotations, rotations, 3, 3, channels, channels)
    group_kernel = jnp.transpose(filter_bank, (0, 4, 1, 5, 2, 3)).reshape(rotations * channels, rotations * channels, 3, 3)
    mixed_sum = conv_full(hidden.astype(jnp.float32).reshape(tile_count, rotations * channels, row_total, col_total), group_kernel)
    mixed_sum = mixed_sum.reshape(tile_count, rotations, channels, row_total, col_total) + group_bias[None, None, :, None, None]
    output = jnp.maximum(mixed_sum, 0.0).astype(jnp.bfloat16)
    return jnp.transpose(output, (1, 2, 3, 0, 4))
```

```python
import functools

import jax
import jax.numpy as jnp
from jax import lax
from jax.experimental import pallas as pl
from jax.experimental.pallas import tpu as pltpu
from jax.sharding import PartitionSpec as P

MESH = pl.DeviceIdType.MESH
STEP = 2


def send_order(chunks):
    inner = list(range(1, chunks - 1))
    return inner[:2] + [0, chunks - 1] + inner[2:]


def mix_order(chunks):
    got, done, plan = set(), set(), []
    for j in send_order(chunks):
        got.add(j)
        ready = [
            i
            for i in range(1, chunks - 1)
            if i not in done and {i - 1, i, i + 1} <= got
        ]
        done.update(ready)
        plan.append((j, ready))
    plan[-1][1].extend([0, chunks - 1])
    return plan


def kernel(
    rots,
    spaces,
    coarse_ref,
    raster_ref,
    lift_ref,
    lift_bias_ref,
    filter_ref,
    group_bias_ref,
    out_ref,
    hid,
    rext,
    filters,
    stacked,
    acc,
    part_out,
    part_in,
    hid_s,
    hid_r,
    up_s,
    up_r,
    down_s,
    down_r,
    ras_s,
    ras_r,
    fil_s,
    fil_r,
    par_s,
    par_r,
):
    g = lax.axis_index("rot")
    s = lax.axis_index("space")
    half = rots // 2
    tiles, rows, ch, cols = coarse_ref.shape
    chunks = rows // STEP
    hi, lo = g // half, lax.rem(g, half)

    def low(k):
        return hi * half + lax.rem(lo + k, half)

    def high(k):
        return lax.rem(g + k * half, rots)

    def gather_group(t):
        return (low, half) if t % 2 == 0 else (high, 2)

    def sum_group(t):
        return (high, 2) if t % 2 == 0 else (low, half)

    has_up = s > 0
    has_down = s < spaces - 1

    def hidden_copy(t, k, j):
        member, n = gather_group(t)
        span = pl.ds(1 + j * STEP, STEP)
        return pltpu.make_async_remote_copy(
            src_ref=hid.at[t, 0, span],
            dst_ref=hid.at[t, n - k, span],
            send_sem=hid_s.at[t, k - 1, j],
            recv_sem=hid_r.at[t, n - k - 1, j],
            device_id=(member(k), s),
            device_id_type=MESH,
        )

    def up_copy(t, k):
        return pltpu.make_async_remote_copy(
            src_ref=hid.at[t, k, 1],
            dst_ref=hid.at[t, k, rows + 1],
            send_sem=up_s.at[t, k],
            recv_sem=up_r.at[t, k],
            device_id=(g, s - 1),
            device_id_type=MESH,
        )

    def down_copy(t, k):
        return pltpu.make_async_remote_copy(
            src_ref=hid.at[t, k, rows],
            dst_ref=hid.at[t, k, 0],
            send_sem=down_s.at[t, k],
            recv_sem=down_r.at[t, k],
            device_id=(g, s + 1),
            device_id_type=MESH,
        )

    def raster_copy(way):
        src, dst, to = ((1, rows + 1, s - 1), (rows, 0, s + 1))[way]
        return pltpu.make_async_remote_copy(
            src_ref=rext.at[src],
            dst_ref=rext.at[dst],
            send_sem=ras_s.at[way],
            recv_sem=ras_r.at[way],
            device_id=(g, to),
            device_id_type=MESH,
        )

    def filter_copy(k):
        return pltpu.make_async_remote_copy(
            src_ref=filter_ref,
            dst_ref=filters.at[rots - k],
            send_sem=fil_s.at[k - 1],
            recv_sem=fil_r.at[rots - k - 1],
            device_id=(lax.rem(g + k, rots), s),
            device_id_type=MESH,
        )

    def part_copy(t, k, j):
        member, n = sum_group(t)
        span = pl.ds(j * STEP, STEP)
        return pltpu.make_async_remote_copy(
            src_ref=part_out.at[t, k - 1, span],
            dst_ref=part_in.at[t, n - k - 1, span],
            send_sem=par_s.at[t, k - 1, j],
            recv_sem=par_r.at[t, n - k - 1, j],
            device_id=(member(k), s),
            device_id_type=MESH,
        )

    barrier = pltpu.get_barrier_semaphore()
    for k in range(1, rots):
        pl.semaphore_signal(barrier, inc=1, device_id=(lax.rem(g + k, rots), s), device_id_type=MESH)

    @pl.when(has_up)
    def _():
        pl.semaphore_signal(barrier, inc=1, device_id=(g, s - 1), device_id_type=MESH)

    @pl.when(has_down)
    def _():
        pl.semaphore_signal(barrier, inc=1, device_id=(g, s + 1), device_id_type=MESH)

    rext[1 : rows + 1] = raster_ref[...]
    zero_row = jnp.zeros((ch, cols), hid.dtype)

    @pl.when(jnp.logical_not(has_up))
    def _():
        rext[0] = jnp.zeros(rext.shape[1:], rext.dtype)
        for t in range(tiles):
            for k in range(gather_group(t)[1]):
                hid[t, k, 0] = zero_row

    @pl.when(jnp.logical_not(has_down))
    def _():
        rext[rows + 1] = jnp.zeros(rext.shape[1:], rext.dtype)
        for t in range(tiles):
            for k in range(gather_group(t)[1]):
                hid[t, k, rows + 1] = zero_row

    around = has_up.astype(jnp.int32) + has_down.astype(jnp.int32)
    pl.semaphore_wait(barrier, rots - 1 + around)

    @pl.when(has_up)
    def _():
        raster_copy(0).start()

    @pl.when(has_down)
    def _():
        raster_copy(1).start()

    def lift_row(r, carry):
        taps = rext[pl.ds(r, 3)].reshape(3 * rext.shape[1], rext.shape[2])
        lifted = jnp.dot(lift_ref[...], taps, preferred_element_type=jnp.float32)
        for t in range(tiles):
            total = lifted[:, t * cols : (t + 1) * cols] + lift_bias_ref[...]
            total = total + coarse_ref[t, r].astype(jnp.float32)
            hid[t, 0, r + 1] = jnp.maximum(total, 0.0).astype(hid.dtype)
        return carry

    for place, j in enumerate(send_order(chunks)):
        if place == 2:

            @pl.when(has_down)
            def _():
                raster_copy(0).wait_recv()

            @pl.when(has_up)
            def _():
                raster_copy(1).wait_recv()

        lax.fori_loop(j * STEP, (j + 1) * STEP, lift_row, 0)
        for t in range(tiles):
            for k in range(1, gather_group(t)[1]):
                hidden_copy(t, k, j).start()
        if place == 1:
            for k in range(1, rots):
                filter_copy(k).start()
        if j == 0:

            @pl.when(has_up)
            def _():
                for t in range(tiles):
                    up_copy(t, 0).start()

        if j == chunks - 1:

            @pl.when(has_down)
            def _():
                for t in range(tiles):
                    down_copy(t, 0).start()

    filters[0] = filter_ref[...]
    for k in range(1, rots):
        filter_copy(k).wait()
    height = filter_ref.shape[0]
    for t in range(tiles):
        take, n_take = gather_group(t)
        give, n_give = sum_group(t)
        for h in range(n_take):
            for p in range(n_give):
                relative = lax.rem(give(p) - take(h) + rots, rots)
                place = lax.rem(relative - g + rots, rots)
                stacked[t, h, p * height : (p + 1) * height] = filters[place]

    lane = lax.broadcasted_iota(jnp.int32, (ch, cols), 1)

    def mix(t, j):
        n_take = gather_group(t)[1]
        n_give = sum_group(t)[1]

        def one_row(r, carry):
            total = None
            for h in range(n_take):
                rim = hid[t, h, pl.ds(r, 3)].reshape(3 * ch, cols)
                term = jnp.dot(
                    stacked[t, h, : n_give * height], rim, preferred_element_type=jnp.float32
                )
                total = term if total is None else total + term
            for p in range(n_give):
                left = total[p * height : p * height + ch]
                mid = total[p * height + ch : p * height + 2 * ch]
                right = total[p * height + 2 * ch : (p + 1) * height]
                left = jnp.where(lane == 0, 0.0, pltpu.roll(left, 1, 1))
                right = jnp.where(lane == cols - 1, 0.0, pltpu.roll(right, cols - 1, 1))
                value = mid + left + right
                if p == 0:
                    acc[t, r] = value + group_bias_ref[...]
                else:
                    part_out[t, p - 1, r] = value.astype(part_out.dtype)
            return carry

        lax.fori_loop(j * STEP, (j + 1) * STEP, one_row, 0)
        for k in range(1, n_give):
            part_copy(t, k, j).start()

    finished = []
    for j, ready in mix_order(chunks):
        for t in range(tiles):
            n_take = gather_group(t)[1]
            for k in range(1, n_take):
                hidden_copy(t, k, j).wait_recv()
            if j == 0:

                @pl.when(has_up)
                def _():
                    for k in range(1, n_take):
                        up_copy(t, k).start()

            if j == chunks - 1:

                @pl.when(has_down)
                def _():
                    for k in range(1, n_take):
                        down_copy(t, k).start()

        for i in ready:
            for t in range(tiles):
                n_take = gather_group(t)[1]
                if i == 0:

                    @pl.when(has_up)
                    def _():
                        for k in range(n_take):
                            down_copy(t, k).wait_recv()

                if i == chunks - 1:

                    @pl.when(has_down)
                    def _():
                        for k in range(n_take):
                            up_copy(t, k).wait_recv()

                mix(t, i)
            finished.append(i)

    for j in finished:
        for t in range(tiles):
            n_give = sum_group(t)[1]
            for k in range(1, n_give):
                part_copy(t, k, j).wait_recv()

            def last_row(r, carry):
                total = acc[t, r]
                for k in range(1, n_give):
                    total = total + part_in[t, k - 1, r].astype(jnp.float32)
                out_ref[t, r] = jnp.maximum(total, 0.0).astype(out_ref.dtype)
                return carry

            lax.fori_loop(j * STEP, (j + 1) * STEP, last_row, 0)

    for t in range(tiles):
        for j in range(chunks):
            for k in range(1, gather_group(t)[1]):
                hidden_copy(t, k, j).wait_send()
            for k in range(1, sum_group(t)[1]):
                part_copy(t, k, j).wait_send()

    @pl.when(has_up)
    def _():
        raster_copy(0).wait_send()
        for t in range(tiles):
            for k in range(gather_group(t)[1]):
                up_copy(t, k).wait_send()

    @pl.when(has_down)
    def _():
        raster_copy(1).wait_send()
        for t in range(tiles):
            for k in range(gather_group(t)[1]):
                down_copy(t, k).wait_send()


def shards(rots, spaces, raster, coarse, lift_weight, lift_bias, group_weight, group_bias):
    ch, cin = lift_weight.shape[2:]
    _, rows, tiles, cols = raster.shape
    half = rots // 2
    most = max(half, 2)
    coarse_in = jnp.transpose(coarse[0], (2, 1, 0, 3))
    wide = jnp.pad(raster, ((0, 0), (0, 0), (0, 0), (1, 1)))
    taps = jnp.stack([wide[..., d : d + cols] for d in range(3)], 0)
    depth = -(-3 * cin // 16) * 16
    taps = jnp.transpose(taps, (2, 0, 1, 3, 4)).reshape(rows, 3 * cin, tiles * cols)
    taps = jnp.pad(taps, ((0, 0), (0, depth - 3 * cin), (0, 0)))
    lift = jnp.transpose(lift_weight[0].reshape(3, 3, ch, cin), (2, 0, 1, 3)).reshape(ch, 3, 3 * cin)
    lift = jnp.pad(lift, ((0, 0), (0, 0), (0, depth - 3 * cin))).reshape(ch, 3 * depth)
    filt = jnp.transpose(group_weight[0].reshape(3, 3, ch, ch), (1, 2, 0, 3)).reshape(3 * ch, 3 * ch)
    bf16, f32 = jnp.bfloat16, jnp.float32
    chunks = rows // STEP
    dma = pltpu.SemaphoreType.DMA
    out = pl.pallas_call(
        functools.partial(kernel, rots, spaces),
        out_shape=jax.ShapeDtypeStruct((tiles, rows, ch, cols), bf16),
        in_specs=[pl.BlockSpec(memory_space=pltpu.VMEM)] * 6,
        out_specs=pl.BlockSpec(memory_space=pltpu.VMEM),
        scratch_shapes=[
            pltpu.VMEM((tiles, most, rows + 2, ch, cols), bf16),
            pltpu.VMEM((rows + 2, depth, tiles * cols), bf16),
            pltpu.VMEM((rots, 3 * ch, 3 * ch), bf16),
            pltpu.VMEM((tiles, most, most * 3 * ch, 3 * ch), bf16),
            pltpu.VMEM((tiles, rows, ch, cols), f32),
            pltpu.VMEM((tiles, most - 1, rows, ch, cols), bf16),
            pltpu.VMEM((tiles, most - 1, rows, ch, cols), bf16),
            dma((tiles, most - 1, chunks)),
            dma((tiles, most - 1, chunks)),
            dma((tiles, most)),
            dma((tiles, most)),
            dma((tiles, most)),
            dma((tiles, most)),
            dma((2,)),
            dma((2,)),
            dma((rots - 1,)),
            dma((rots - 1,)),
            dma((tiles, most - 1, chunks)),
            dma((tiles, most - 1, chunks)),
        ],
        compiler_params=pltpu.CompilerParams(
            collective_id=0, has_side_effects=True, vmem_limit_bytes=48 * 2**20
        ),
        name="mixing_layers",
    )(coarse_in, taps, lift, lift_bias[:, None], filt, group_bias[:, None])
    return jnp.transpose(out, (2, 1, 0, 3))[None]


def solution(mesh):
    return jax.shard_map(
        functools.partial(shards, mesh.shape["rot"], mesh.shape["space"]),
        mesh=mesh,
        in_specs=(
            P(None, "space", None, None),
            P("rot", None, "space", None, None),
            P("rot", None, None, None),
            P(),
            P("rot", None, None, None),
            P(),
        ),
        out_specs=P("rot", None, "space", None, None),
        check_vma=False,
    )
```

```python
import functools

import jax
import jax.numpy as jnp
from jax import lax
from jax.experimental import pallas as pl
from jax.experimental.pallas import tpu as pltpu
from jax.sharding import PartitionSpec as P

MESH = pl.DeviceIdType.MESH
STEP = 2


def send_order(chunks):
    return [1, 2, 0, chunks - 1, chunks - 2] + list(range(3, chunks - 2))


def mix_order(chunks):
    got, done, plan = set(), set(), []
    for place, j in enumerate(send_order(chunks)):
        got.add(j)
        ready = [
            i
            for i in range(1, chunks - 1)
            if i not in done and {i - 1, i, i + 1} <= got
        ]
        done.update(ready)
        if place == 4:
            ready.append(0)
        if place == 5:
            ready.append(chunks - 1)
        plan.append((j, ready))
    return plan


def column(row):
    n = row.shape[1]
    shape = (n, n)
    same = lax.broadcasted_iota(jnp.int32, shape, 0) == lax.broadcasted_iota(jnp.int32, shape, 1)
    return jnp.sum(jnp.where(same, row, 0.0), axis=1, keepdims=True)


def packed_filter(weight_ref):
    w = [weight_ref[i] for i in range(9)]
    half = w[0].shape[0] // 2
    parts = [jnp.concatenate([w[dx], w[3 + dx]], 1) for dx in range(3)]
    late = jnp.concatenate(w[6:], 0)
    parts.append(jnp.concatenate([late[: 3 * half], late[3 * half :]], 1))
    return jnp.concatenate(parts, 0)


def opened_filter(packed):
    lanes = packed.shape[1] // 2
    top = packed[: 6 * lanes // 2]
    late = packed[6 * lanes // 2 :]
    return jnp.concatenate([top, jnp.concatenate([late[:, :lanes], late[:, lanes:]], 0)], 1)


def kernel(
    rots,
    spaces,
    coarse_ref,
    raster_ref,
    lift_ref,
    lift_bias_ref,
    filter_ref,
    group_bias_ref,
    out_ref,
    hid,
    rext,
    packed,
    filters,
    stacked,
    acc,
    part_out,
    part_in,
    hid_s,
    hid_r,
    up_s,
    up_r,
    down_s,
    down_r,
    ras_s,
    ras_r,
    fil_s,
    fil_r,
    mate_s,
    mate_r,
    par_s,
    par_r,
):
    g = lax.axis_index("rot")
    s = lax.axis_index("space")
    half = rots // 2
    tiles, rows, ch, cols = coarse_ref.shape
    chunks = rows // STEP
    hi, lo = g // half, lax.rem(g, half)

    def low(k):
        return hi * half + lax.rem(lo + k, half)

    def high(k):
        return lax.rem(g + k * half, rots)

    def gather_group(t):
        return (low, half) if t % 2 == 0 else (high, 2)

    def sum_group(t):
        return (high, 2) if t % 2 == 0 else (low, half)

    has_up = s > 0
    has_down = s < spaces - 1

    def hidden_copy(t, k, j):
        member, n = gather_group(t)
        span = pl.ds(1 + j * STEP, STEP)
        return pltpu.make_async_remote_copy(
            src_ref=hid.at[t, 0, span],
            dst_ref=hid.at[t, n - k, span],
            send_sem=hid_s.at[t, k - 1, j],
            recv_sem=hid_r.at[t, n - k - 1, j],
            device_id=(member(k), s),
            device_id_type=MESH,
        )

    def up_copy(t, k):
        return pltpu.make_async_remote_copy(
            src_ref=hid.at[t, k, 1],
            dst_ref=hid.at[t, k, rows + 1],
            send_sem=up_s.at[t, k],
            recv_sem=up_r.at[t, k],
            device_id=(g, s - 1),
            device_id_type=MESH,
        )

    def down_copy(t, k):
        return pltpu.make_async_remote_copy(
            src_ref=hid.at[t, k, rows],
            dst_ref=hid.at[t, k, 0],
            send_sem=down_s.at[t, k],
            recv_sem=down_r.at[t, k],
            device_id=(g, s + 1),
            device_id_type=MESH,
        )

    def raster_copy(way):
        src, dst, to = ((1, rows + 1, s - 1), (rows, 0, s + 1))[way]
        return pltpu.make_async_remote_copy(
            src_ref=rext.at[src],
            dst_ref=rext.at[dst],
            send_sem=ras_s.at[way],
            recv_sem=ras_r.at[way],
            device_id=(g, to),
            device_id_type=MESH,
        )

    side = lax.rem(s, 2)

    def filter_copy(k):
        return pltpu.make_async_remote_copy(
            src_ref=packed.at[0, side],
            dst_ref=packed.at[rots - k, side],
            send_sem=fil_s.at[k - 1],
            recv_sem=fil_r.at[rots - k - 1],
            device_id=(lax.rem(g + k, rots), s),
            device_id_type=MESH,
        )

    def mate_copy(k):
        return pltpu.make_async_remote_copy(
            src_ref=packed.at[k, side],
            dst_ref=packed.at[k, side],
            send_sem=mate_s.at[k - 1],
            recv_sem=mate_r.at[k - 1],
            device_id=(g, s + 1 - 2 * side),
            device_id_type=MESH,
        )

    def part_copy(t, k, j):
        member, n = sum_group(t)
        span = pl.ds(j * STEP, STEP)
        return pltpu.make_async_remote_copy(
            src_ref=part_out.at[t, k - 1, span],
            dst_ref=part_in.at[t, n - k - 1, span],
            send_sem=par_s.at[t, k - 1, j],
            recv_sem=par_r.at[t, n - k - 1, j],
            device_id=(member(k), s),
            device_id_type=MESH,
        )

    barrier = pltpu.get_barrier_semaphore()
    for k in range(1, rots):
        pl.semaphore_signal(barrier, inc=1, device_id=(lax.rem(g + k, rots), s), device_id_type=MESH)

    @pl.when(has_up)
    def _():
        pl.semaphore_signal(barrier, inc=1, device_id=(g, s - 1), device_id_type=MESH)

    @pl.when(has_down)
    def _():
        pl.semaphore_signal(barrier, inc=1, device_id=(g, s + 1), device_id_type=MESH)

    rext[1 : rows + 1] = raster_ref[...]
    packed[0] = packed_filter(filter_ref).reshape(packed.shape[1:])
    zero_row = jnp.zeros((ch, cols), hid.dtype)

    @pl.when(jnp.logical_not(has_up))
    def _():
        rext[0] = jnp.zeros(rext.shape[1:], rext.dtype)
        for t in range(tiles):
            for k in range(gather_group(t)[1]):
                hid[t, k, 0] = zero_row

    @pl.when(jnp.logical_not(has_down))
    def _():
        rext[rows + 1] = jnp.zeros(rext.shape[1:], rext.dtype)
        for t in range(tiles):
            for k in range(gather_group(t)[1]):
                hid[t, k, rows + 1] = zero_row

    around = has_up.astype(jnp.int32) + has_down.astype(jnp.int32)
    pl.semaphore_wait(barrier, rots - 1 + around)

    @pl.when(has_up)
    def _():
        raster_copy(0).start()

    @pl.when(has_down)
    def _():
        raster_copy(1).start()

    for k in range(1, rots):
        filter_copy(k).start()

    lift_bias = column(lift_bias_ref[...])
    group_bias = column(group_bias_ref[...])

    def lift_row(r, carry):
        taps = rext[pl.ds(r, 3)].reshape(3 * rext.shape[1], rext.shape[2])
        lifted = jnp.dot(lift_ref[...], taps, preferred_element_type=jnp.float32)
        for t in range(tiles):
            total = lifted[:, t * cols : (t + 1) * cols] + lift_bias
            total = total + coarse_ref[t, r].astype(jnp.float32)
            hid[t, 0, r + 1] = jnp.maximum(total, 0.0).astype(hid.dtype)
        return carry

    for place, j in enumerate(send_order(chunks)):
        if place == 2:

            @pl.when(has_down)
            def _():
                raster_copy(0).wait_recv()

            @pl.when(has_up)
            def _():
                raster_copy(1).wait_recv()

        lax.fori_loop(j * STEP, (j + 1) * STEP, lift_row, 0, unroll=True)
        for t in range(tiles):
            for k in range(1, gather_group(t)[1]):
                hidden_copy(t, k, j).start()
        if j == 0:

            @pl.when(has_up)
            def _():
                for t in range(tiles):
                    up_copy(t, 0).start()

        if j == chunks - 1:

            @pl.when(has_down)
            def _():
                for t in range(tiles):
                    down_copy(t, 0).start()

    for k in range(1, rots):
        filter_copy(k).wait_recv()
        mate_copy(rots - k).start()
    filters[0] = opened_filter(packed[0].reshape(-1, packed.shape[3]))
    for k in range(1, rots):
        mate_copy(k).wait_recv()
        filters[k] = opened_filter(packed[k].reshape(-1, packed.shape[3]))
    height = filters.shape[1]
    for t in range(tiles):
        take, n_take = gather_group(t)
        give, n_give = sum_group(t)
        for h in range(n_take):
            for p in range(n_give):
                relative = lax.rem(give(p) - take(h) + rots, rots)
                place = lax.rem(relative - g + rots, rots)
                stacked[t, h, p * height : (p + 1) * height] = filters[place]

    lane = lax.broadcasted_iota(jnp.int32, (ch, cols), 1)

    def mix(t, j):
        n_take = gather_group(t)[1]
        n_give = sum_group(t)[1]

        def one_row(r, carry):
            total = None
            for h in range(n_take):
                rim = hid[t, h, pl.ds(r, 3)].reshape(3 * ch, cols)
                term = jnp.dot(
                    stacked[t, h, : n_give * height], rim, preferred_element_type=jnp.float32
                )
                total = term if total is None else total + term
            for p in range(n_give):
                left = total[p * height : p * height + ch]
                mid = total[p * height + ch : p * height + 2 * ch]
                right = total[p * height + 2 * ch : (p + 1) * height]
                left = jnp.where(lane == 0, 0.0, pltpu.roll(left, 1, 1))
                right = jnp.where(lane == cols - 1, 0.0, pltpu.roll(right, cols - 1, 1))
                value = mid + left + right
                if p == 0:
                    acc[t, r] = value + group_bias
                else:
                    part_out[t, p - 1, r] = value.astype(part_out.dtype)
            return carry

        lax.fori_loop(j * STEP, (j + 1) * STEP, one_row, 0, unroll=True)
        for k in range(1, n_give):
            part_copy(t, k, j).start()

    finished = []
    for j, ready in mix_order(chunks):
        for t in range(tiles):
            n_take = gather_group(t)[1]
            for k in range(1, n_take):
                hidden_copy(t, k, j).wait_recv()
            if j == 0:

                @pl.when(has_up)
                def _():
                    for k in range(1, n_take):
                        up_copy(t, k).start()

            if j == chunks - 1:

                @pl.when(has_down)
                def _():
                    for k in range(1, n_take):
                        down_copy(t, k).start()

        for i in ready:
            for t in range(tiles):
                n_take = gather_group(t)[1]
                if i == 0:

                    @pl.when(has_up)
                    def _():
                        for k in range(n_take):
                            down_copy(t, k).wait_recv()

                if i == chunks - 1:

                    @pl.when(has_down)
                    def _():
                        for k in range(n_take):
                            up_copy(t, k).wait_recv()

                mix(t, i)
            finished.append(i)

    for j in finished:
        for t in range(tiles):
            n_give = sum_group(t)[1]
            for k in range(1, n_give):
                part_copy(t, k, j).wait_recv()

            def last_row(r, carry):
                total = acc[t, r]
                for k in range(1, n_give):
                    total = total + part_in[t, k - 1, r].astype(jnp.float32)
                out_ref[t, r] = jnp.maximum(total, 0.0).astype(out_ref.dtype)
                return carry

            lax.fori_loop(j * STEP, (j + 1) * STEP, last_row, 0, unroll=True)

    for k in range(1, rots):
        filter_copy(k).wait_send()
        mate_copy(k).wait_send()
    for t in range(tiles):
        for j in range(chunks):
            for k in range(1, gather_group(t)[1]):
                hidden_copy(t, k, j).wait_send()
            for k in range(1, sum_group(t)[1]):
                part_copy(t, k, j).wait_send()

    @pl.when(has_up)
    def _():
        raster_copy(0).wait_send()
        for t in range(tiles):
            for k in range(gather_group(t)[1]):
                up_copy(t, k).wait_send()

    @pl.when(has_down)
    def _():
        raster_copy(1).wait_send()
        for t in range(tiles):
            for k in range(gather_group(t)[1]):
                down_copy(t, k).wait_send()


def shards(rots, spaces, raster, coarse, lift_weight, lift_bias, group_weight, group_bias):
    ch, cin = lift_weight.shape[2:]
    _, rows, tiles, cols = raster.shape
    half = rots // 2
    most = max(half, 2)
    coarse_in = jnp.transpose(coarse[0], (2, 1, 0, 3))
    wide = jnp.pad(raster, ((0, 0), (0, 0), (0, 0), (1, 1)))
    taps = jnp.stack([wide[..., d : d + cols] for d in range(3)], 0)
    depth = -(-3 * cin // 16) * 16
    taps = jnp.transpose(taps, (2, 0, 1, 3, 4)).reshape(rows, 3 * cin, tiles * cols)
    taps = jnp.pad(taps, ((0, 0), (0, depth - 3 * cin), (0, 0)))
    lift = jnp.transpose(lift_weight[0].reshape(3, 3, ch, cin), (2, 0, 1, 3)).reshape(ch, 3, 3 * cin)
    lift = jnp.pad(lift, ((0, 0), (0, 0), (0, depth - 3 * cin))).reshape(ch, 3 * depth)
    bf16, f32 = jnp.bfloat16, jnp.float32
    chunks = rows // STEP
    dma = pltpu.SemaphoreType.DMA
    out = pl.pallas_call(
        functools.partial(kernel, rots, spaces),
        out_shape=jax.ShapeDtypeStruct((tiles, rows, ch, cols), bf16),
        in_specs=[pl.BlockSpec(memory_space=pltpu.VMEM)] * 6,
        out_specs=pl.BlockSpec(memory_space=pltpu.VMEM),
        scratch_shapes=[
            pltpu.VMEM((tiles, most, rows + 2, ch, cols), bf16),
            pltpu.VMEM((rows + 2, depth, tiles * cols), bf16),
            pltpu.VMEM((rots, 2, 9 * ch // 4, 2 * ch), bf16),
            pltpu.VMEM((rots, 3 * ch, 3 * ch), bf16),
            pltpu.VMEM((tiles, most, most * 3 * ch, 3 * ch), bf16),
            pltpu.VMEM((tiles, rows, ch, cols), f32),
            pltpu.VMEM((tiles, most - 1, rows, ch, cols), bf16),
            pltpu.VMEM((tiles, most - 1, rows, ch, cols), bf16),
            dma((tiles, most - 1, chunks)),
            dma((tiles, most - 1, chunks)),
            dma((tiles, most)),
            dma((tiles, most)),
            dma((tiles, most)),
            dma((tiles, most)),
            dma((2,)),
            dma((2,)),
            dma((rots - 1,)),
            dma((rots - 1,)),
            dma((rots - 1,)),
            dma((rots - 1,)),
            dma((tiles, most - 1, chunks)),
            dma((tiles, most - 1, chunks)),
        ],
        compiler_params=pltpu.CompilerParams(
            collective_id=0, has_side_effects=True, vmem_limit_bytes=48 * 2**20
        ),
        name="mixing_layers",
    )(coarse_in, taps, lift, lift_bias[None], group_weight[0], group_bias[None])
    return jnp.transpose(out, (2, 1, 0, 3))[None]


def solution(mesh):
    return jax.shard_map(
        functools.partial(shards, mesh.shape["rot"], mesh.shape["space"]),
        mesh=mesh,
        in_specs=(
            P(None, "space", None, None),
            P("rot", None, "space", None, None),
            P("rot", None, None, None),
            P(),
            P("rot", None, None, None),
            P(),
        ),
        out_specs=P("rot", None, "space", None, None),
        check_vma=False,
    )
```

```python
import functools

import jax
import jax.numpy as jnp
from jax import lax
from jax.experimental import pallas as pl
from jax.experimental.pallas import tpu as pltpu
from jax.sharding import PartitionSpec as P

MESH = pl.DeviceIdType.MESH
STEP = 2


def send_order(chunks):
    return [1, 2, 0, chunks - 1, chunks - 2] + list(range(3, chunks - 2))


def mix_order(chunks):
    got, done, plan = set(), set(), []
    for place, j in enumerate(send_order(chunks)):
        got.add(j)
        ready = [
            i
            for i in range(1, chunks - 1)
            if i not in done and {i - 1, i, i + 1} <= got
        ]
        done.update(ready)
        if place == 4:
            ready.append(0)
        if place == 5:
            ready.append(chunks - 1)
        plan.append((j, ready))
    return plan


def column(row):
    n = row.shape[1]
    shape = (n, n)
    same = lax.broadcasted_iota(jnp.int32, shape, 0) == lax.broadcasted_iota(jnp.int32, shape, 1)
    return jnp.sum(jnp.where(same, row, 0.0), axis=1, keepdims=True)


def packed_filter(weight_ref):
    w = [weight_ref[i] for i in range(9)]
    half = w[0].shape[0] // 2
    parts = [jnp.concatenate([w[dx], w[3 + dx]], 1) for dx in range(3)]
    late = jnp.concatenate(w[6:], 0)
    parts.append(jnp.concatenate([late[: 3 * half], late[3 * half :]], 1))
    return jnp.concatenate(parts, 0)


def opened_filter(packed):
    lanes = packed.shape[1] // 2
    top = packed[: 6 * lanes // 2]
    late = packed[6 * lanes // 2 :]
    return jnp.concatenate([top, jnp.concatenate([late[:, :lanes], late[:, lanes:]], 0)], 1)


def kernel(
    rots,
    spaces,
    cin,
    coarse_ref,
    raster_ref,
    lift_ref,
    lift_bias_hbm,
    filter_hbm,
    group_bias_hbm,
    out_ref,
    lift_bias_ref,
    filter_ref,
    group_bias_ref,
    load_s,
    hid,
    rext,
    packed,
    filters,
    stacked,
    acc,
    part_out,
    part_in,
    hid_s,
    hid_r,
    up_s,
    up_r,
    down_s,
    down_r,
    ras_s,
    ras_r,
    fil_s,
    fil_r,
    mate_s,
    mate_r,
    par_s,
    par_r,
):
    g = lax.axis_index("rot")
    s = lax.axis_index("space")
    half = rots // 2
    tiles, rows, ch, cols = coarse_ref.shape
    chunks = rows // STEP
    hi, lo = g // half, lax.rem(g, half)

    def low(k):
        return hi * half + lax.rem(lo + k, half)

    def high(k):
        return lax.rem(g + k * half, rots)

    def gather_group(t):
        return (low, half) if t % 2 == 0 else (high, 2)

    def sum_group(t):
        return (high, 2) if t % 2 == 0 else (low, half)

    has_up = s > 0
    has_down = s < spaces - 1

    def hidden_copy(t, k, j):
        member, n = gather_group(t)
        span = pl.ds(1 + j * STEP, STEP)
        return pltpu.make_async_remote_copy(
            src_ref=hid.at[t, 0, span],
            dst_ref=hid.at[t, n - k, span],
            send_sem=hid_s.at[t, k - 1, j],
            recv_sem=hid_r.at[t, n - k - 1, j],
            device_id=(member(k), s),
            device_id_type=MESH,
        )

    def up_copy(t, k):
        return pltpu.make_async_remote_copy(
            src_ref=hid.at[t, k, 1],
            dst_ref=hid.at[t, k, rows + 1],
            send_sem=up_s.at[t, k],
            recv_sem=up_r.at[t, k],
            device_id=(g, s - 1),
            device_id_type=MESH,
        )

    def down_copy(t, k):
        return pltpu.make_async_remote_copy(
            src_ref=hid.at[t, k, rows],
            dst_ref=hid.at[t, k, 0],
            send_sem=down_s.at[t, k],
            recv_sem=down_r.at[t, k],
            device_id=(g, s + 1),
            device_id_type=MESH,
        )

    def raster_copy(way):
        src, dst, to = ((1, rows + 1, s - 1), (rows, 0, s + 1))[way]
        return pltpu.make_async_remote_copy(
            src_ref=rext.at[src],
            dst_ref=rext.at[dst],
            send_sem=ras_s.at[way],
            recv_sem=ras_r.at[way],
            device_id=(g, to),
            device_id_type=MESH,
        )

    side = lax.rem(s, 2)

    def filter_copy(k):
        return pltpu.make_async_remote_copy(
            src_ref=packed.at[0, side],
            dst_ref=packed.at[rots - k, side],
            send_sem=fil_s.at[k - 1],
            recv_sem=fil_r.at[rots - k - 1],
            device_id=(lax.rem(g + k, rots), s),
            device_id_type=MESH,
        )

    def mate_copy(k):
        return pltpu.make_async_remote_copy(
            src_ref=packed.at[k, side],
            dst_ref=packed.at[k, side],
            send_sem=mate_s.at[k - 1],
            recv_sem=mate_r.at[k - 1],
            device_id=(g, s + 1 - 2 * side),
            device_id_type=MESH,
        )

    def part_copy(t, k, j):
        member, n = sum_group(t)
        span = pl.ds(j * STEP, STEP)
        return pltpu.make_async_remote_copy(
            src_ref=part_out.at[t, k - 1, span],
            dst_ref=part_in.at[t, n - k - 1, span],
            send_sem=par_s.at[t, k - 1, j],
            recv_sem=par_r.at[t, n - k - 1, j],
            device_id=(member(k), s),
            device_id_type=MESH,
        )

    barrier = pltpu.get_barrier_semaphore()
    for k in range(1, rots):
        pl.semaphore_signal(barrier, inc=1, device_id=(lax.rem(g + k, rots), s), device_id_type=MESH)

    @pl.when(has_up)
    def _():
        pl.semaphore_signal(barrier, inc=1, device_id=(g, s - 1), device_id_type=MESH)

    @pl.when(has_down)
    def _():
        pl.semaphore_signal(barrier, inc=1, device_id=(g, s + 1), device_id_type=MESH)

    loads = [
        pltpu.make_async_copy(source, target, load_s.at[i])
        for i, (source, target) in enumerate(
            (
                (filter_hbm, filter_ref),
                (lift_bias_hbm, lift_bias_ref),
                (group_bias_hbm, group_bias_ref),
            )
        )
    ]
    for load in loads:
        load.start()

    pixel = lax.broadcasted_iota(jnp.int32, raster_ref.shape[1:], 1)
    wide = tiles * cols

    def spread_row(r, carry):
        mid = raster_ref[r].astype(jnp.float32)
        left = jnp.where(pixel % cols == 0, 0.0, pltpu.roll(mid, 1, 1))
        right = jnp.where(pixel % cols == cols - 1, 0.0, pltpu.roll(mid, wide - 1, 1))
        taps = left + pltpu.roll(mid, cin, 0) + pltpu.roll(right, 2 * cin, 0)
        rext[r + 1] = taps.astype(rext.dtype)
        return carry

    lax.fori_loop(0, rows, spread_row, 0, unroll=True)
    for load in loads:
        load.wait()
    packed[0] = packed_filter(filter_ref).reshape(packed.shape[1:])
    zero_row = jnp.zeros((ch, cols), hid.dtype)

    @pl.when(jnp.logical_not(has_up))
    def _():
        rext[0] = jnp.zeros(rext.shape[1:], rext.dtype)
        for t in range(tiles):
            for k in range(gather_group(t)[1]):
                hid[t, k, 0] = zero_row

    @pl.when(jnp.logical_not(has_down))
    def _():
        rext[rows + 1] = jnp.zeros(rext.shape[1:], rext.dtype)
        for t in range(tiles):
            for k in range(gather_group(t)[1]):
                hid[t, k, rows + 1] = zero_row

    around = has_up.astype(jnp.int32) + has_down.astype(jnp.int32)
    pl.semaphore_wait(barrier, rots - 1 + around)

    @pl.when(has_up)
    def _():
        raster_copy(0).start()

    @pl.when(has_down)
    def _():
        raster_copy(1).start()

    for k in range(1, rots):
        filter_copy(k).start()

    lift_bias = column(lift_bias_ref[...])
    group_bias = column(group_bias_ref[...])

    def lift_row(r, carry):
        taps = rext[pl.ds(r, 3)].reshape(3 * rext.shape[1], rext.shape[2])
        lifted = jnp.dot(lift_ref[...], taps, preferred_element_type=jnp.float32)
        for t in range(tiles):
            total = lifted[:, t * cols : (t + 1) * cols] + lift_bias
            total = total + coarse_ref[t, r].astype(jnp.float32)
            hid[t, 0, r + 1] = jnp.maximum(total, 0.0).astype(hid.dtype)
        return carry

    for place, j in enumerate(send_order(chunks)):
        if place == 2:

            @pl.when(has_down)
            def _():
                raster_copy(0).wait_recv()

            @pl.when(has_up)
            def _():
                raster_copy(1).wait_recv()

        lax.fori_loop(j * STEP, (j + 1) * STEP, lift_row, 0, unroll=True)
        for t in range(tiles):
            for k in range(1, gather_group(t)[1]):
                hidden_copy(t, k, j).start()
        if j == 0:

            @pl.when(has_up)
            def _():
                for t in range(tiles):
                    up_copy(t, 0).start()

        if j == chunks - 1:

            @pl.when(has_down)
            def _():
                for t in range(tiles):
                    down_copy(t, 0).start()

    for k in range(1, rots):
        filter_copy(k).wait_recv()
        mate_copy(rots - k).start()
    filters[0] = opened_filter(packed[0].reshape(-1, packed.shape[3]))
    for k in range(1, rots):
        mate_copy(k).wait_recv()
        filters[k] = opened_filter(packed[k].reshape(-1, packed.shape[3]))
    height = filters.shape[1]
    for t in range(tiles):
        take, n_take = gather_group(t)
        give, n_give = sum_group(t)
        for h in range(n_take):
            for p in range(n_give):
                relative = lax.rem(give(p) - take(h) + rots, rots)
                place = lax.rem(relative - g + rots, rots)
                stacked[t, h, p * height : (p + 1) * height] = filters[place]

    lane = lax.broadcasted_iota(jnp.int32, (ch, cols), 1)

    def mix(t, j):
        n_take = gather_group(t)[1]
        n_give = sum_group(t)[1]

        def one_row(r, carry):
            total = None
            for h in range(n_take):
                rim = hid[t, h, pl.ds(r, 3)].reshape(3 * ch, cols)
                term = jnp.dot(
                    stacked[t, h, : n_give * height], rim, preferred_element_type=jnp.float32
                )
                total = term if total is None else total + term
            for p in range(n_give):
                left = total[p * height : p * height + ch]
                mid = total[p * height + ch : p * height + 2 * ch]
                right = total[p * height + 2 * ch : (p + 1) * height]
                left = jnp.where(lane == 0, 0.0, pltpu.roll(left, 1, 1))
                right = jnp.where(lane == cols - 1, 0.0, pltpu.roll(right, cols - 1, 1))
                value = mid + left + right
                if p == 0:
                    acc[t, r] = value + group_bias
                else:
                    part_out[t, p - 1, r] = value.astype(part_out.dtype)
            return carry

        lax.fori_loop(j * STEP, (j + 1) * STEP, one_row, 0, unroll=True)
        for k in range(1, n_give):
            part_copy(t, k, j).start()

    finished = []
    for j, ready in mix_order(chunks):
        for t in range(tiles):
            n_take = gather_group(t)[1]
            for k in range(1, n_take):
                hidden_copy(t, k, j).wait_recv()
            if j == 0:

                @pl.when(has_up)
                def _():
                    for k in range(1, n_take):
                        up_copy(t, k).start()

            if j == chunks - 1:

                @pl.when(has_down)
                def _():
                    for k in range(1, n_take):
                        down_copy(t, k).start()

        for i in ready:
            for t in range(tiles):
                n_take = gather_group(t)[1]
                if i == 0:

                    @pl.when(has_up)
                    def _():
                        for k in range(n_take):
                            down_copy(t, k).wait_recv()

                if i == chunks - 1:

                    @pl.when(has_down)
                    def _():
                        for k in range(n_take):
                            up_copy(t, k).wait_recv()

                mix(t, i)
            finished.append(i)

    for j in finished:
        for t in range(tiles):
            n_give = sum_group(t)[1]
            for k in range(1, n_give):
                part_copy(t, k, j).wait_recv()

        for r in range(j * STEP, (j + 1) * STEP):
            totals = []
            for t in range(tiles):
                total = acc[t, r]
                for k in range(1, sum_group(t)[1]):
                    total = total + part_in[t, k - 1, r].astype(jnp.float32)
                totals.append(jnp.maximum(total, 0.0))
            out_ref[:, r] = jnp.stack(totals, 1).astype(out_ref.dtype)

    for k in range(1, rots):
        filter_copy(k).wait_send()
        mate_copy(k).wait_send()
    for t in range(tiles):
        for j in range(chunks):
            for k in range(1, gather_group(t)[1]):
                hidden_copy(t, k, j).wait_send()
            for k in range(1, sum_group(t)[1]):
                part_copy(t, k, j).wait_send()

    @pl.when(has_up)
    def _():
        raster_copy(0).wait_send()
        for t in range(tiles):
            for k in range(gather_group(t)[1]):
                up_copy(t, k).wait_send()

    @pl.when(has_down)
    def _():
        raster_copy(1).wait_send()
        for t in range(tiles):
            for k in range(gather_group(t)[1]):
                down_copy(t, k).wait_send()


def shards(rots, spaces, raster, coarse, lift_weight, lift_bias, group_weight, group_bias):
    ch, cin = lift_weight.shape[2:]
    _, rows, tiles, cols = raster.shape
    half = rots // 2
    most = max(half, 2)
    coarse_in = jnp.transpose(coarse[0], (2, 1, 0, 3))
    depth = -(-3 * cin // 16) * 16
    taps = jnp.transpose(raster, (1, 0, 2, 3)).reshape(rows, cin, tiles * cols)
    taps = jnp.pad(taps, ((0, 0), (0, depth - cin), (0, 0)))
    lift = jnp.transpose(lift_weight[0].reshape(3, 3, ch, cin), (2, 0, 1, 3)).reshape(ch, 3, 3 * cin)
    lift = jnp.pad(lift, ((0, 0), (0, 0), (0, depth - 3 * cin))).reshape(ch, 3 * depth)
    bf16, f32 = jnp.bfloat16, jnp.float32
    chunks = rows // STEP
    dma = pltpu.SemaphoreType.DMA
    out = pl.pallas_call(
        functools.partial(kernel, rots, spaces, cin),
        out_shape=jax.ShapeDtypeStruct((ch, rows, tiles, cols), bf16),
        in_specs=[pl.BlockSpec(memory_space=pltpu.VMEM)] * 3
        + [pl.BlockSpec(memory_space=pl.ANY)] * 3,
        out_specs=pl.BlockSpec(memory_space=pltpu.VMEM),
        scratch_shapes=[
            pltpu.VMEM((1, ch), f32),
            pltpu.VMEM((9, ch, ch), bf16),
            pltpu.VMEM((1, ch), f32),
            dma((3,)),
            pltpu.VMEM((tiles, most, rows + 2, ch, cols), bf16),
            pltpu.VMEM((rows + 2, depth, tiles * cols), bf16),
            pltpu.VMEM((rots, 2, 9 * ch // 4, 2 * ch), bf16),
            pltpu.VMEM((rots, 3 * ch, 3 * ch), bf16),
            pltpu.VMEM((tiles, most, most * 3 * ch, 3 * ch), bf16),
            pltpu.VMEM((tiles, rows, ch, cols), f32),
            pltpu.VMEM((tiles, most - 1, rows, ch, cols), bf16),
            pltpu.VMEM((tiles, most - 1, rows, ch, cols), bf16),
            dma((tiles, most - 1, chunks)),
            dma((tiles, most - 1, chunks)),
            dma((tiles, most)),
            dma((tiles, most)),
            dma((tiles, most)),
            dma((tiles, most)),
            dma((2,)),
            dma((2,)),
            dma((rots - 1,)),
            dma((rots - 1,)),
            dma((rots - 1,)),
            dma((rots - 1,)),
            dma((tiles, most - 1, chunks)),
            dma((tiles, most - 1, chunks)),
        ],
        compiler_params=pltpu.CompilerParams(
            collective_id=0, has_side_effects=True, vmem_limit_bytes=48 * 2**20
        ),
        name="mixing_layers",
    )(coarse_in, taps, lift, lift_bias[None], group_weight[0], group_bias[None])
    return out[None]


def solution(mesh):
    return jax.shard_map(
        functools.partial(shards, mesh.shape["rot"], mesh.shape["space"]),
        mesh=mesh,
        in_specs=(
            P(None, "space", None, None),
            P("rot", None, "space", None, None),
            P("rot", None, None, None),
            P(),
            P("rot", None, None, None),
            P(),
        ),
        out_specs=P("rot", None, "space", None, None),
        check_vma=False,
    )
```

```python
import functools

import jax
import jax.numpy as jnp
from jax import lax
from jax.experimental import pallas as pl
from jax.experimental.pallas import tpu as pltpu
from jax.sharding import PartitionSpec as P

MESH = pl.DeviceIdType.MESH
STEP = 2


def send_order(chunks):
    return [1, 2, 0, chunks - 1, chunks - 2] + list(range(3, chunks - 2))


def mix_order(chunks):
    got, done, plan = set(), set(), []
    for place, j in enumerate(send_order(chunks)):
        got.add(j)
        ready = [
            i
            for i in range(1, chunks - 1)
            if i not in done and {i - 1, i, i + 1} <= got
        ]
        done.update(ready)
        if place == 4:
            ready.append(0)
        if place == 5:
            ready.append(chunks - 1)
        plan.append((j, ready))
    return plan


def column(row):
    n = row.shape[1]
    shape = (n, n)
    same = lax.broadcasted_iota(jnp.int32, shape, 0) == lax.broadcasted_iota(jnp.int32, shape, 1)
    return jnp.sum(jnp.where(same, row, 0.0), axis=1, keepdims=True)


def packed_filter(weight_ref):
    w = [weight_ref[i] for i in range(9)]
    half = w[0].shape[0] // 2
    parts = [jnp.concatenate([w[dx], w[3 + dx]], 1) for dx in range(3)]
    late = jnp.concatenate(w[6:], 0)
    parts.append(jnp.concatenate([late[: 3 * half], late[3 * half :]], 1))
    return jnp.concatenate(parts, 0)


def opened_filter(packed):
    lanes = packed.shape[1] // 2
    top = packed[: 6 * lanes // 2]
    late = packed[6 * lanes // 2 :]
    return jnp.concatenate([top, jnp.concatenate([late[:, :lanes], late[:, lanes:]], 0)], 1)


def kernel(
    rots,
    spaces,
    cin,
    coarse_ref,
    raster_ref,
    lift_ref,
    lift_bias_hbm,
    filter_hbm,
    group_bias_hbm,
    out_ref,
    lift_bias_ref,
    filter_ref,
    group_bias_ref,
    load_s,
    hid,
    rext,
    packed,
    filters,
    stacked,
    acc,
    part_out,
    part_in,
    hid_s,
    hid_r,
    up_s,
    up_r,
    down_s,
    down_r,
    ras_s,
    ras_r,
    fil_s,
    fil_r,
    mate_s,
    mate_r,
    par_s,
    par_r,
):
    g = lax.axis_index("rot")
    s = lax.axis_index("space")
    half = rots // 2
    ch, rows, tiles, cols = coarse_ref.shape
    chunks = rows // STEP
    hi, lo = g // half, lax.rem(g, half)

    def low(k):
        return hi * half + lax.rem(lo + k, half)

    def high(k):
        return lax.rem(g + k * half, rots)

    def gather_group(t):
        return (low, half) if t % 2 == 0 else (high, 2)

    def sum_group(t):
        return (high, 2) if t % 2 == 0 else (low, half)

    has_up = s > 0
    has_down = s < spaces - 1

    def hidden_copy(t, k, j):
        member, n = gather_group(t)
        span = pl.ds(1 + j * STEP, STEP)
        return pltpu.make_async_remote_copy(
            src_ref=hid.at[t, 0, span],
            dst_ref=hid.at[t, n - k, span],
            send_sem=hid_s.at[t, k - 1, j],
            recv_sem=hid_r.at[t, n - k - 1, j],
            device_id=(member(k), s),
            device_id_type=MESH,
        )

    def up_copy(t, k):
        return pltpu.make_async_remote_copy(
            src_ref=hid.at[t, k, 1],
            dst_ref=hid.at[t, k, rows + 1],
            send_sem=up_s.at[t, k],
            recv_sem=up_r.at[t, k],
            device_id=(g, s - 1),
            device_id_type=MESH,
        )

    def down_copy(t, k):
        return pltpu.make_async_remote_copy(
            src_ref=hid.at[t, k, rows],
            dst_ref=hid.at[t, k, 0],
            send_sem=down_s.at[t, k],
            recv_sem=down_r.at[t, k],
            device_id=(g, s + 1),
            device_id_type=MESH,
        )

    def raster_copy(way):
        src, dst, to = ((1, rows + 1, s - 1), (rows, 0, s + 1))[way]
        return pltpu.make_async_remote_copy(
            src_ref=rext.at[src],
            dst_ref=rext.at[dst],
            send_sem=ras_s.at[way],
            recv_sem=ras_r.at[way],
            device_id=(g, to),
            device_id_type=MESH,
        )

    side = lax.rem(s, 2)

    def filter_copy(k):
        return pltpu.make_async_remote_copy(
            src_ref=packed.at[0, side],
            dst_ref=packed.at[rots - k, side],
            send_sem=fil_s.at[k - 1],
            recv_sem=fil_r.at[rots - k - 1],
            device_id=(lax.rem(g + k, rots), s),
            device_id_type=MESH,
        )

    def mate_copy(k):
        return pltpu.make_async_remote_copy(
            src_ref=packed.at[k, side],
            dst_ref=packed.at[k, side],
            send_sem=mate_s.at[k - 1],
            recv_sem=mate_r.at[k - 1],
            device_id=(g, s + 1 - 2 * side),
            device_id_type=MESH,
        )

    def part_copy(t, k, j):
        member, n = sum_group(t)
        span = pl.ds(j * STEP, STEP)
        return pltpu.make_async_remote_copy(
            src_ref=part_out.at[t, k - 1, span],
            dst_ref=part_in.at[t, n - k - 1, span],
            send_sem=par_s.at[t, k - 1, j],
            recv_sem=par_r.at[t, n - k - 1, j],
            device_id=(member(k), s),
            device_id_type=MESH,
        )

    barrier = pltpu.get_barrier_semaphore()
    for k in range(1, rots):
        pl.semaphore_signal(barrier, inc=1, device_id=(lax.rem(g + k, rots), s), device_id_type=MESH)

    @pl.when(has_up)
    def _():
        pl.semaphore_signal(barrier, inc=1, device_id=(g, s - 1), device_id_type=MESH)

    @pl.when(has_down)
    def _():
        pl.semaphore_signal(barrier, inc=1, device_id=(g, s + 1), device_id_type=MESH)

    loads = [
        pltpu.make_async_copy(source, target, load_s.at[i])
        for i, (source, target) in enumerate(
            (
                (filter_hbm, filter_ref),
                (lift_bias_hbm, lift_bias_ref),
                (group_bias_hbm, group_bias_ref),
            )
        )
    ]
    for load in loads:
        load.start()

    pixel = lax.broadcasted_iota(jnp.int32, raster_ref.shape[1:], 1)
    wide = tiles * cols

    def spread_row(r, carry):
        mid = raster_ref[r].astype(jnp.float32)
        left = jnp.where(pixel % cols == 0, 0.0, pltpu.roll(mid, 1, 1))
        right = jnp.where(pixel % cols == cols - 1, 0.0, pltpu.roll(mid, wide - 1, 1))
        taps = left + pltpu.roll(mid, cin, 0) + pltpu.roll(right, 2 * cin, 0)
        rext[r + 1] = taps.astype(rext.dtype)
        return carry

    lax.fori_loop(0, rows, spread_row, 0, unroll=True)
    for load in loads:
        load.wait()
    packed[0] = packed_filter(filter_ref).reshape(packed.shape[1:])
    zero_row = jnp.zeros((ch, cols), hid.dtype)

    @pl.when(jnp.logical_not(has_up))
    def _():
        rext[0] = jnp.zeros(rext.shape[1:], rext.dtype)
        for t in range(tiles):
            for k in range(gather_group(t)[1]):
                hid[t, k, 0] = zero_row

    @pl.when(jnp.logical_not(has_down))
    def _():
        rext[rows + 1] = jnp.zeros(rext.shape[1:], rext.dtype)
        for t in range(tiles):
            for k in range(gather_group(t)[1]):
                hid[t, k, rows + 1] = zero_row

    around = has_up.astype(jnp.int32) + has_down.astype(jnp.int32)
    pl.semaphore_wait(barrier, rots - 1 + around)

    @pl.when(has_up)
    def _():
        raster_copy(0).start()

    @pl.when(has_down)
    def _():
        raster_copy(1).start()

    for k in range(1, rots):
        filter_copy(k).start()

    lift_bias = column(lift_bias_ref[...])
    group_bias = column(group_bias_ref[...])

    def lift_row(r, carry):
        taps = rext[pl.ds(r, 3)].reshape(3 * rext.shape[1], rext.shape[2])
        lifted = jnp.dot(lift_ref[...], taps, preferred_element_type=jnp.float32)
        both = coarse_ref[:, r].astype(jnp.float32)
        for t in range(tiles):
            total = lifted[:, t * cols : (t + 1) * cols] + lift_bias
            total = total + both[:, t]
            hid[t, 0, r + 1] = jnp.maximum(total, 0.0).astype(hid.dtype)
        return carry

    for place, j in enumerate(send_order(chunks)):
        if place == 2:

            @pl.when(has_down)
            def _():
                raster_copy(0).wait_recv()

            @pl.when(has_up)
            def _():
                raster_copy(1).wait_recv()

        lax.fori_loop(j * STEP, (j + 1) * STEP, lift_row, 0, unroll=True)
        for t in range(tiles):
            for k in range(1, gather_group(t)[1]):
                hidden_copy(t, k, j).start()
        if j == 0:

            @pl.when(has_up)
            def _():
                for t in range(tiles):
                    up_copy(t, 0).start()

        if j == chunks - 1:

            @pl.when(has_down)
            def _():
                for t in range(tiles):
                    down_copy(t, 0).start()

    for k in range(1, rots):
        filter_copy(k).wait_recv()
        mate_copy(rots - k).start()
    filters[0] = opened_filter(packed[0].reshape(-1, packed.shape[3]))
    for k in range(1, rots):
        mate_copy(k).wait_recv()
        filters[k] = opened_filter(packed[k].reshape(-1, packed.shape[3]))
    height = filters.shape[1]
    for t in range(tiles):
        take, n_take = gather_group(t)
        give, n_give = sum_group(t)
        for h in range(n_take):
            for p in range(n_give):
                relative = lax.rem(give(p) - take(h) + rots, rots)
                place = lax.rem(relative - g + rots, rots)
                stacked[t, h, p * height : (p + 1) * height] = filters[place]

    lane = lax.broadcasted_iota(jnp.int32, (ch, cols), 1)

    def mix(t, j):
        n_take = gather_group(t)[1]
        n_give = sum_group(t)[1]

        def one_row(r, carry):
            total = None
            for h in range(n_take):
                rim = hid[t, h, pl.ds(r, 3)].reshape(3 * ch, cols)
                term = jnp.dot(
                    stacked[t, h, : n_give * height], rim, preferred_element_type=jnp.float32
                )
                total = term if total is None else total + term
            for p in range(n_give):
                left = total[p * height : p * height + ch]
                mid = total[p * height + ch : p * height + 2 * ch]
                right = total[p * height + 2 * ch : (p + 1) * height]
                left = jnp.where(lane == 0, 0.0, pltpu.roll(left, 1, 1))
                right = jnp.where(lane == cols - 1, 0.0, pltpu.roll(right, cols - 1, 1))
                value = mid + left + right
                if p == 0:
                    acc[t, r] = value + group_bias
                else:
                    part_out[t, p - 1, r] = value.astype(part_out.dtype)
            return carry

        lax.fori_loop(j * STEP, (j + 1) * STEP, one_row, 0, unroll=True)
        for k in range(1, n_give):
            part_copy(t, k, j).start()

    finished = []
    for j, ready in mix_order(chunks):
        for t in range(tiles):
            n_take = gather_group(t)[1]
            for k in range(1, n_take):
                hidden_copy(t, k, j).wait_recv()
            if j == 0:

                @pl.when(has_up)
                def _():
                    for k in range(1, n_take):
                        up_copy(t, k).start()

            if j == chunks - 1:

                @pl.when(has_down)
                def _():
                    for k in range(1, n_take):
                        down_copy(t, k).start()

        for i in ready:
            for t in range(tiles):
                n_take = gather_group(t)[1]
                if i == 0:

                    @pl.when(has_up)
                    def _():
                        for k in range(n_take):
                            down_copy(t, k).wait_recv()

                if i == chunks - 1:

                    @pl.when(has_down)
                    def _():
                        for k in range(n_take):
                            up_copy(t, k).wait_recv()

                mix(t, i)
            finished.append(i)

    for j in finished:
        for t in range(tiles):
            n_give = sum_group(t)[1]
            for k in range(1, n_give):
                part_copy(t, k, j).wait_recv()

        for r in range(j * STEP, (j + 1) * STEP):
            totals = []
            for t in range(tiles):
                total = acc[t, r]
                for k in range(1, sum_group(t)[1]):
                    total = total + part_in[t, k - 1, r].astype(jnp.float32)
                totals.append(jnp.maximum(total, 0.0))
            out_ref[:, r] = jnp.stack(totals, 1).astype(out_ref.dtype)

    for k in range(1, rots):
        filter_copy(k).wait_send()
        mate_copy(k).wait_send()
    for t in range(tiles):
        for j in range(chunks):
            for k in range(1, gather_group(t)[1]):
                hidden_copy(t, k, j).wait_send()
            for k in range(1, sum_group(t)[1]):
                part_copy(t, k, j).wait_send()

    @pl.when(has_up)
    def _():
        raster_copy(0).wait_send()
        for t in range(tiles):
            for k in range(gather_group(t)[1]):
                up_copy(t, k).wait_send()

    @pl.when(has_down)
    def _():
        raster_copy(1).wait_send()
        for t in range(tiles):
            for k in range(gather_group(t)[1]):
                down_copy(t, k).wait_send()


def shards(rots, spaces, raster, coarse, lift_weight, lift_bias, group_weight, group_bias):
    ch, cin = lift_weight.shape[2:]
    _, rows, tiles, cols = raster.shape
    half = rots // 2
    most = max(half, 2)
    depth = -(-3 * cin // 16) * 16
    taps = jnp.transpose(raster, (1, 0, 2, 3)).reshape(rows, cin, tiles * cols)
    taps = jnp.pad(taps, ((0, 0), (0, depth - cin), (0, 0)))
    lift = jnp.transpose(lift_weight[0].reshape(3, 3, ch, cin), (2, 0, 1, 3)).reshape(ch, 3, 3 * cin)
    lift = jnp.pad(lift, ((0, 0), (0, 0), (0, depth - 3 * cin))).reshape(ch, 3 * depth)
    bf16, f32 = jnp.bfloat16, jnp.float32
    chunks = rows // STEP
    dma = pltpu.SemaphoreType.DMA
    out = pl.pallas_call(
        functools.partial(kernel, rots, spaces, cin),
        out_shape=jax.ShapeDtypeStruct((ch, rows, tiles, cols), bf16),
        in_specs=[pl.BlockSpec(memory_space=pltpu.VMEM)] * 3
        + [pl.BlockSpec(memory_space=pl.ANY)] * 3,
        out_specs=pl.BlockSpec(memory_space=pltpu.VMEM),
        scratch_shapes=[
            pltpu.VMEM((1, ch), f32),
            pltpu.VMEM((9, ch, ch), bf16),
            pltpu.VMEM((1, ch), f32),
            dma((3,)),
            pltpu.VMEM((tiles, most, rows + 2, ch, cols), bf16),
            pltpu.VMEM((rows + 2, depth, tiles * cols), bf16),
            pltpu.VMEM((rots, 2, 9 * ch // 4, 2 * ch), bf16),
            pltpu.VMEM((rots, 3 * ch, 3 * ch), bf16),
            pltpu.VMEM((tiles, most, most * 3 * ch, 3 * ch), bf16),
            pltpu.VMEM((tiles, rows, ch, cols), f32),
            pltpu.VMEM((tiles, most - 1, rows, ch, cols), bf16),
            pltpu.VMEM((tiles, most - 1, rows, ch, cols), bf16),
            dma((tiles, most - 1, chunks)),
            dma((tiles, most - 1, chunks)),
            dma((tiles, most)),
            dma((tiles, most)),
            dma((tiles, most)),
            dma((tiles, most)),
            dma((2,)),
            dma((2,)),
            dma((rots - 1,)),
            dma((rots - 1,)),
            dma((rots - 1,)),
            dma((rots - 1,)),
            dma((tiles, most - 1, chunks)),
            dma((tiles, most - 1, chunks)),
        ],
        compiler_params=pltpu.CompilerParams(
            collective_id=0, has_side_effects=True, vmem_limit_bytes=48 * 2**20
        ),
        name="mixing_layers",
    )(coarse[0], taps, lift, lift_bias[None], group_weight[0], group_bias[None])
    return out[None]


def solution(mesh):
    return jax.shard_map(
        functools.partial(shards, mesh.shape["rot"], mesh.shape["space"]),
        mesh=mesh,
        in_specs=(
            P(None, "space", None, None),
            P("rot", None, "space", None, None),
            P("rot", None, None, None),
            P(),
            P("rot", None, None, None),
            P(),
        ),
        out_specs=P("rot", None, "space", None, None),
        check_vma=False,
    )
```
